32 devices in a mesh: groups: 2 (over y), dp: 8 (over z, x), tensor: 2 (over core).
Axes of the slice: x: 2, y: 2, z: 4, core: 2. Of those that a mesh axis runs over, the one named last changes fastest.
Arguments:
- inputs_t: bfloat16 [8192, 2048], P('tensor', ('groups', 'dp')), parts along dimension 1, may hold values from -6 to 6
- cotangent_t: bfloat16 [8192, 2048], P('tensor', ('groups', 'dp')), parts along dimension 1, may hold values from -6 to 6
- adapter_down: bfloat16 [128, 16, 8192], P(('groups', 'dp'), None, 'tensor'), parts along dimension 0, may hold values from -0.0625 to 0.0625
- adapter_up: bfloat16 [128, 16, 8192], P(('groups', 'dp'), None, 'tensor'), parts along dimension 0, may hold values from -1.5 to 1.5
- block_tenant: int32 [16], P(('groups', 'dp')), parts along dimension 0, may hold values from 0 to 63
- block_rows: int32 [16], P(('groups', 'dp')), parts along dimension 0, may hold values from 0 to 128, as said below
- owner_slot: int32 [128], P('groups'), parts along dimension 0, may hold values from 0 to 63, as said below
Outputs:
- delta_t: bfloat16 [8192, 2048], P('tensor', ('groups', 'dp')), parts along dimension 1
- grad_input_t: bfloat16 [8192, 2048], P('tensor', ('groups', 'dp')), parts along dimension 1
- grad_down: float32 [128, 16, 8192], P(('groups', 'dp'), None, 'tensor'), parts along dimension 0
- grad_up: float32 [128, 16, 8192], P(('groups', 'dp'), None, 'tensor'), parts along dimension 0
The draws below stay inside these ranges and needn't reach their ends.
There are 2 independent parts, one for each index of `groups`. The reference program is written for one: setup_inputs(seed, part) draws one part's arguments, and reference() takes and returns one part's arrays. A program takes and returns all parts, laid end to end along the dimension named above; each array names one. Nothing has to cross between parts.
Inputs may be any that keep to these rules, and one draw needn't show every extreme that they name: `block_rows`: each block's count of live token slots; live slots come first in a block. `owner_slot`: distinct slots, one for each tenant.
All inputs are finite; a program needn't handle non-finite values.
Results may differ from the reference program's by a relative error of at most 0.0051.
Values may be sent and summed in bfloat16 or wider, within the bound.
A program may use at most 64 MiB of HBM per device.

```python
import math
import jax
import jax.numpy as jnp
import numpy as np
from jax import lax

D = 8192
TENANTS = 64
RANK = 16
BLOCK = 128
SLOTS = 1
TOKENS = 1024
OWNER_SLOTS = 64
N_DP = 8


def draw_block_rows(key, part):
    key = jax.random.fold_in(key, 11)
    first_key, second_key = jax.random.split(key)
    level = jax.random.randint(first_key, (N_DP, 1), 0, 4)
    raw_rows = jax.random.randint(second_key, (N_DP, SLOTS), 0, BLOCK + 1)
    counted = jnp.minimum(BLOCK, raw_rows * (level + 1) // 2).reshape(-1)
    counted = counted.at[0].set(BLOCK)
    counted = counted.at[N_DP * SLOTS - 1].set(0)
    return counted.astype(jnp.int32)


def draw_owner_slot(key, part):
    key = jax.random.fold_in(key, 23)
    first_key, second_key = jax.random.split(key)
    inner = 1 + jax.random.permutation(first_key, OWNER_SLOTS - 2)
    listed = jnp.concatenate([jnp.array([0, OWNER_SLOTS - 1], dtype=jnp.int32), inner[:TENANTS - 2].astype(jnp.int32)])
    order = jax.random.permutation(second_key, TENANTS)
    return listed[order].astype(jnp.int32)


def set_ends(drawn, rng, smallest, top_value):
    extent = drawn.shape
    place = [jax.random.randint(jax.random.fold_in(rng, axis), (), 0, extent[axis]) for axis in range(len(extent))]
    drawn = drawn.at[tuple(place)].set(smallest)
    longest = extent.index(max(extent))
    place[longest] = (place[longest] + 1) % extent[longest]
    return drawn.at[tuple(place)].set(top_value)


def block_levels(stream_key, extent, pieces, smallest, largest):
    gain = 1.0
    for axis_at, blocks in pieces:
        steps = jax.random.uniform(jax.random.fold_in(jax.random.fold_in(stream_key, 6), axis_at), (blocks,), jnp.float32, smallest / len(pieces), largest / len(pieces))
        gain = gain * jnp.repeat(jnp.exp(steps), extent[axis_at] // blocks).reshape((-1,) + (1,) * (len(extent) - 1 - axis_at))
    return gain


def cumulative_ranks(number_of, slope):
    portions = [(1 << 20) // math.isqrt(rank ** slope) + 1 for rank in range(1, number_of + 1)]
    width = 1 + sum(portions) // (1 << 30)
    return np.cumsum(np.array([max(1, weight // width) for weight in portions]))


def skewed_ids(own_key, extent, count, skew):
    listing = cumulative_ranks(count, skew)
    pick = jax.random.randint(jax.random.fold_in(own_key, 1), extent, 0, int(listing[count - 1]))
    standing = jnp.searchsorted(jnp.asarray(listing, jnp.int32), pick, side="right")
    return jax.random.permutation(jax.random.fold_in(own_key, 2), count)[standing].astype(jnp.int32)


def normal_values(rng, dims, deviation, most, shards=(), held_as=jnp.bfloat16):
    result = jax.random.normal(rng, dims, jnp.float32) * deviation
    if len(shards) > 0:
        result = block_levels(rng, dims, shards, -0.22, 0.18) * result
    return jnp.clip(result, min=-most, max=most).astype(held_as)


def setup_inputs(seed: int = 0, part: int = 0) -> dict:
    key_of = jax.random.split(jax.random.key(seed), 8)
    own_keys = jax.random.split(jax.random.fold_in(key_of[7], part), 8)
    inputs_t = normal_values(own_keys[0], (D, TOKENS), 1.0, 6.0, ((0, 2), (1, 8)))
    cotangent_t = normal_values(own_keys[1], (D, TOKENS), 1.0, 6.0, ((0, 2), (1, 8)))
    adapter_down = normal_values(own_keys[2], (OWNER_SLOTS, RANK, D), D ** -0.5, 0.0625, ((0, 8), (2, 2)))
    adapter_up = normal_values(own_keys[3], (OWNER_SLOTS, RANK, D), RANK ** -0.5, 1.5, ((0, 8), (2, 2)))
    block_tenant = set_ends(skewed_ids(own_keys[4], (TOKENS // BLOCK,), TENANTS, 2), jax.random.fold_in(own_keys[4], 3), 0, TENANTS - 1).astype(jnp.int32)
    block_rows = draw_block_rows(jax.random.fold_in(jax.random.fold_in(key_of[7], part), 71), part)
    owner_slot = draw_owner_slot(jax.random.fold_in(jax.random.fold_in(key_of[7], part), 71), part)
    return dict(inputs_t=inputs_t, cotangent_t=cotangent_t, adapter_down=adapter_down, adapter_up=adapter_up, block_tenant=block_tenant, block_rows=block_rows, owner_slot=owner_slot)


adapter_scale_factor = 2.0
grad_scale = 0.125


def reference(inputs_t, cotangent_t, adapter_down, adapter_up, block_tenant, block_rows, owner_slot):
    features, columns = inputs_t.shape
    block_count = columns // BLOCK
    positions = jnp.arange(columns, dtype=jnp.int32)
    valid = (positions % BLOCK) < jnp.repeat(block_rows, BLOCK, total_repeat_length=columns)
    keeping = valid.astype(jnp.bfloat16)
    masked_in = inputs_t * keeping[None, :]
    masked_grad = cotangent_t * keeping[None, :]
    block_slot = owner_slot[block_tenant].astype(jnp.int32)
    empty_grads = jnp.zeros(adapter_down.shape, jnp.float32)

    def one_block(totals, block_index):
        sum_down, sum_up = totals
        first_col = (block_index * BLOCK).astype(jnp.int32)
        token_block = lax.dynamic_slice_in_dim(masked_in, first_col, BLOCK, 1)
        grad_block = lax.dynamic_slice_in_dim(masked_grad, first_col, BLOCK, 1)
        slot_id = block_slot[block_index]
        down_weight_rows = adapter_down[slot_id]
        up_weight_rows = adapter_up[slot_id]
        rounded_low_rank = jnp.dot(down_weight_rows, token_block, preferred_element_type=jnp.float32).astype(jnp.bfloat16)
        backward_rounded = jnp.dot(up_weight_rows, grad_block, preferred_element_type=jnp.float32).astype(jnp.bfloat16)
        block_update = (adapter_scale_factor * jnp.dot(up_weight_rows.T, rounded_low_rank, preferred_element_type=jnp.float32)).astype(jnp.bfloat16)
        block_input_rows = (adapter_scale_factor * jnp.dot(down_weight_rows.T, backward_rounded, preferred_element_type=jnp.float32)).astype(jnp.bfloat16)
        sum_down = sum_down.at[slot_id].add(jnp.dot(backward_rounded, token_block.T, preferred_element_type=jnp.float32))
        sum_up = sum_up.at[slot_id].add(jnp.dot(rounded_low_rank, grad_block.T, preferred_element_type=jnp.float32))
        return (sum_down, sum_up), (block_update, block_input_rows)

    (sum_down, sum_up), (deltas, input_terms) = lax.scan(
        one_block, (empty_grads, empty_grads), jnp.arange(block_count, dtype=jnp.int32))
    delta_t = jnp.transpose(deltas, (1, 0, 2)).reshape(features, columns)
    grad_input_t = jnp.transpose(input_terms, (1, 0, 2)).reshape(features, columns)
    return delta_t, grad_input_t, grad_scale * sum_down, grad_scale * sum_up
```

```python
import functools
import jax
import jax.numpy as jnp
from jax import lax
from jax.experimental import pallas as pl
from jax.experimental.pallas import tpu as pltpu
from jax.sharding import PartitionSpec as P

MESH = pl.DeviceIdType.MESH
BF = jnp.bfloat16
F32 = jnp.float32
CHUNKS = 4
WAYS = ((1, 0), (-1, 1))


def place_of(dev, n):
    odd = lax.rem(dev, 2)
    half = lax.div(dev, 2)
    return (1 - odd) * half + odd * (n - 1 - half)


def dev_of(place, n):
    q = lax.rem(place + 2 * n, n)
    high = lax.div(q, n // 2)
    return (1 - high) * (2 * q) + high * (2 * (n - 1 - q) + 1)


def exchange(
    n,
    tenant_ref, rows_ref, owner_ref, in_hbm, cot_hbm, down_hbm, up_hbm,
    delta_hbm, gin_hbm, terms_hbm, slots_hbm,
    tokens, adapters, slot_src, slots, first, moving, mine, part_mine, part_other, ranks, terms,
    result,
    load_sem, slot_send, slot_recv, rs_send, rs_recv, part_send, part_recv,
    ag_send, ag_recv, keep_sem, out_sem, slot_out, credit,
):
    own, rank, width = down_hbm.shape
    half = width // 2
    depth = moving.shape[2]
    d = lax.axis_index("dp")
    t = lax.axis_index("tensor")
    p = place_of(d, n)
    neighbour = (dev_of(p + 1, n), dev_of(p - 1, n))

    loads = [
        pltpu.make_async_copy(down_hbm, adapters.at[0], load_sem.at[0]),
        pltpu.make_async_copy(up_hbm, adapters.at[1], load_sem.at[1]),
        pltpu.make_async_copy(in_hbm, tokens.at[0], load_sem.at[2]),
        pltpu.make_async_copy(cot_hbm, tokens.at[1], load_sem.at[3]),
    ]
    for load in loads:
        load.start()

    barrier = pltpu.get_barrier_semaphore()

    def greet(i, _):
        pl.semaphore_signal(
            barrier, inc=1, device_id={"dp": lax.rem(d + i, n)}, device_id_type=MESH
        )
        return 0

    lax.fori_loop(1, n, greet, 0)
    pl.semaphore_signal(barrier, inc=1, device_id={"tensor": 1 - t}, device_id_type=MESH)
    my_slot = owner_ref[tenant_ref[0]]
    slot_vec = jnp.full((1, 128), my_slot, jnp.int32)
    slot_src[...] = slot_vec
    slots[d] = slot_vec
    pl.semaphore_wait(barrier, n)

    def slot_copy(i):
        to = lax.rem(d + i, n)
        return pltpu.make_async_remote_copy(
            src_ref=slot_src, dst_ref=slots.at[d],
            send_sem=slot_send.at[i], recv_sem=slot_recv.at[d],
            device_id={"dp": to}, device_id_type=MESH,
        )

    def slot_wait(i):
        who = lax.rem(d + i, n)
        return pltpu.make_async_remote_copy(
            src_ref=slot_src, dst_ref=slots.at[who],
            send_sem=slot_send.at[i], recv_sem=slot_recv.at[who],
            device_id={"dp": who}, device_id_type=MESH,
        )

    lax.fori_loop(1, n, lambda i, c: (slot_copy(i).start(), c)[1], 0)
    loads[0].wait()
    loads[1].wait()
    lax.fori_loop(1, n, lambda i, c: (slot_wait(i).wait_recv(), c)[1], 0)

    def masks(block):
        v = jnp.broadcast_to(slots[block], (rank, 128))
        return [
            jnp.where(v == d * own + j, 1.0, 0.0).astype(F32).astype(BF) for j in range(own)
        ]

    def share(a, r, chosen):
        total = None
        for j in range(own):
            gate = jnp.concatenate([chosen[j]] * (half // 128), axis=1)
            term = gate * adapters[a, j, :, r * half:(r + 1) * half]
            total = term if total is None else total + term
        return total

    def rs_copy(a, r, step, src):
        return pltpu.make_async_remote_copy(
            src_ref=src, dst_ref=moving.at[a, r, lax.rem(step, depth)],
            send_sem=rs_send.at[a, r, lax.rem(step, depth)],
            recv_sem=rs_recv.at[a, r, lax.rem(step, depth)],
            device_id={"dp": neighbour[r]}, device_id_type=MESH,
        )

    def source(a, r, step):
        return moving.at[a, r, lax.rem(step - 1 + depth, depth)]

    for way, r in WAYS:
        chosen = masks(dev_of(p - way, n))
        for a in range(2):
            first[a, r] = share(a, r, chosen)
            rs_copy(a, r, 0, first.at[a, r]).start()

    def rs_step(step, _):
        chosen = [masks(dev_of(p - way * (1 + step), n)) for way, r in WAYS]
        for a in range(2):
            for way, r in WAYS:
                add = share(a, r, chosen[r])
                rs_copy(a, r, step - 1, first.at[a, r]).wait_recv()
                here = lax.rem(step - 1, depth)
                moving[a, r, here] = moving[a, r, here] + add
                if depth < n - 1:
                    rs_copy(a, r, step - 1, first.at[a, r]).wait_send()

                    @pl.when((step >= 2) & (step - 2 <= n - 2 - depth))
                    def _():
                        pl.semaphore_signal(
                            credit.at[a, r], inc=1,
                            device_id={"dp": neighbour[1 - r]}, device_id_type=MESH,
                        )

                    @pl.when(step >= depth)
                    def _():
                        pl.semaphore_wait(credit.at[a, r], 1)

                rs_copy(a, r, step, source(a, r, step)).start()
        return 0

    lax.fori_loop(1, n - 1, rs_step, 0)

    lanes = lax.broadcasted_iota(jnp.int32, (rank, 128), 1)
    keep = jnp.where(lanes < rows_ref[0], 1.0, 0.0).astype(F32)
    loads[2].wait()
    loads[3].wait()
    own_chosen = masks(d)

    def part_copy(a):
        return pltpu.make_async_remote_copy(
            src_ref=part_mine.at[a], dst_ref=part_other.at[a],
            send_sem=part_send.at[a], recv_sem=part_recv.at[a],
            device_id={"tensor": 1 - t}, device_id_type=MESH,
        )

    for a in range(2):
        for way, r in WAYS:
            add = share(a, r, own_chosen)
            rs_copy(a, r, n - 2, first.at[a, r]).wait_recv()
            mine[a, :, r * half:(r + 1) * half] = moving[a, r, (n - 2) % depth] + add
        part_mine[a] = jnp.dot(mine[a], tokens[a], preferred_element_type=F32)
        part_copy(a).start()

    def ag_copy(a, r, step):
        block = dev_of(p - WAYS[r][0] * step, n)
        piece = terms.at[a, block, :, pl.ds(r * half, half)]
        return pltpu.make_async_remote_copy(
            src_ref=piece, dst_ref=piece,
            send_sem=ag_send.at[a, r, step], recv_sem=ag_recv.at[a, r, step],
            device_id={"dp": neighbour[r]}, device_id_type=MESH,
        )

    def ag_arrive(a, r, step):
        block = dev_of(p - WAYS[r][0] * (step + 1), n)
        piece = terms.at[a, block, :, pl.ds(r * half, half)]
        return pltpu.make_async_remote_copy(
            src_ref=piece, dst_ref=piece,
            send_sem=ag_send.at[a, r, step], recv_sem=ag_recv.at[a, r, step],
            device_id={"dp": neighbour[r]}, device_id_type=MESH,
        )

    def keep_copy(a, r, step):
        block = dev_of(p - WAYS[r][0] * step, n)
        return pltpu.make_async_copy(
            terms.at[a, block, :, pl.ds(r * half, half)],
            terms_hbm.at[a, block, :, pl.ds(r * half, half)],
            keep_sem.at[a, r, step],
        )

    for a in range(2):
        part_copy(a).wait_recv()
        ranks[a] = ((part_mine[a] + part_other[a]) * keep).astype(BF)
        for r in range(2):
            terms[a, d, :, r * half:(r + 1) * half] = lax.dot_general(
                ranks[a], tokens[1 - a, r * half:(r + 1) * half, :],
                (((1,), (1,)), ((), ())), preferred_element_type=F32,
            ).astype(BF)
            ag_copy(a, r, 0).start()
            keep_copy(a, r, 0).start()

    size = width // CHUNKS

    def result_copy(a, i):
        at = pl.ds(i * size, size)
        return pltpu.make_async_copy(
            result.at[a, at], (delta_hbm, gin_hbm)[a].at[at], out_sem.at[a, i]
        )

    def result_chunk(i):
        at = slice(i * size, (i + 1) * size)
        for a in range(2):
            twice = ranks[a] + ranks[a]
            result[a, at, :] = lax.dot_general(
                mine[1 - a, :, at], twice,
                (((0,), (0,)), ((), ())), preferred_element_type=F32,
            ).astype(BF)
            result_copy(a, i).start()

    def ag_step(step):
        for a in range(2):
            for r in range(2):
                ag_arrive(a, r, step - 1).wait_recv()
                ag_copy(a, r, step).start()
                keep_copy(a, r, step).start()

    result_chunk(0)
    early = min(CHUNKS, n - 1)
    for step in range(1, early):
        ag_step(step)
        result_chunk(step)
    for i in range(early, CHUNKS):
        result_chunk(i)
    lax.fori_loop(early, n - 1, lambda s, c: (ag_step(s), c)[1], 0)
    slot_keep = pltpu.make_async_copy(slots, slots_hbm, slot_out)
    slot_keep.start()
    for a in range(2):
        for r in range(2):
            ag_arrive(a, r, n - 2).wait_recv()
            keep_copy(a, r, n - 1).start()

    def slot_end(i, c):
        slot_copy(i).wait_send()
        return c

    lax.fori_loop(1, n, slot_end, 0)

    def rs_end(step, c):
        for a in range(2):
            for r in range(2):
                rs_copy(a, r, step, first.at[a, r]).wait_send()
        return c

    lax.fori_loop(n - 2 if depth < n - 1 else 0, n - 1, rs_end, 0)

    def ag_end(step, c):
        for a in range(2):
            for r in range(2):
                ag_copy(a, r, step).wait_send()
        return c

    lax.fori_loop(0, n - 1, ag_end, 0)

    def keep_end(step, c):
        for a in range(2):
            for r in range(2):
                keep_copy(a, r, step).wait()
        return c

    lax.fori_loop(0, n, keep_end, 0)
    for a in range(2):
        part_copy(a).wait_send()
        for i in range(CHUNKS):
            result_copy(a, i).wait()
    slot_keep.wait()


def collect(n, slots_ref, base_ref, terms_ref, down_ref, up_ref):
    own = down_ref.shape[0]
    down_ref[...] = jnp.zeros_like(down_ref)
    up_ref[...] = jnp.zeros_like(up_ref)

    def add(b, c):
        at = slots_ref[b, 0, 0] - base_ref[0]

        @pl.when((at >= 0) & (at < own))
        def _():
            up_ref[at] += 0.125 * terms_ref[0, b].astype(F32)
            down_ref[at] += 0.125 * terms_ref[1, b].astype(F32)

        return c

    lax.fori_loop(0, n, add, 0)


def shards(n, inputs_t, cotangent_t, adapter_down, adapter_up, block_tenant, block_rows, owner_slot):
    width, columns = inputs_t.shape
    own, rank, _ = adapter_down.shape
    half = width // 2
    depth = min(n - 1, 8)
    smem = pl.BlockSpec(memory_space=pltpu.SMEM)
    anyw = pl.BlockSpec(memory_space=pl.ANY)
    dma = pltpu.SemaphoreType.DMA
    delta_t, grad_input_t, terms, slots = pl.pallas_call(
        functools.partial(exchange, n),
        out_shape=(
            jax.ShapeDtypeStruct((width, columns), BF),
            jax.ShapeDtypeStruct((width, columns), BF),
            jax.ShapeDtypeStruct((2, n, rank, width), BF),
            jax.ShapeDtypeStruct((n, 1, 128), jnp.int32),
        ),
        in_specs=[smem, smem, smem, anyw, anyw, anyw, anyw],
        out_specs=(anyw,) * 4,
        scratch_shapes=[
            pltpu.VMEM((2, width, columns), BF),
            pltpu.VMEM((2, own, rank, width), BF),
            pltpu.VMEM((1, 128), jnp.int32),
            pltpu.VMEM((n, 1, 128), jnp.int32),
            pltpu.VMEM((2, 2, rank, half), BF),
            pltpu.VMEM((2, 2, depth, rank, half), BF),
            pltpu.VMEM((2, rank, width), BF),
            pltpu.VMEM((2, rank, columns), F32),
            pltpu.VMEM((2, rank, columns), F32),
            pltpu.VMEM((2, rank, columns), BF),
            pltpu.VMEM((2, n, rank, width), BF),
            pltpu.VMEM((2, width, columns), BF),
            dma((4,)),
            dma((n,)),
            dma((n,)),
            dma((2, 2, depth)),
            dma((2, 2, depth)),
            dma((2,)),
            dma((2,)),
            dma((2, 2, n)),
            dma((2, 2, n)),
            dma((2, 2, n)),
            dma((2, CHUNKS)),
            dma,
            pltpu.SemaphoreType.REGULAR((2, 2)),
        ],
        compiler_params=pltpu.CompilerParams(
            collective_id=0, has_side_effects=True, vmem_limit_bytes=56 * 1024 * 1024
        ),
        name="exchange",
    )(block_tenant, block_rows, owner_slot, inputs_t, cotangent_t, adapter_down, adapter_up)
    base = jnp.full((1,), lax.axis_index("dp") * own, jnp.int32)
    tile = min(width, 512)
    grad_down, grad_up = pl.pallas_call(
        functools.partial(collect, n),
        grid=(width // tile,),
        out_shape=(
            jax.ShapeDtypeStruct((own, rank, width), F32),
            jax.ShapeDtypeStruct((own, rank, width), F32),
        ),
        in_specs=[smem, smem, pl.BlockSpec((2, n, rank, tile), lambda i: (0, 0, 0, i))],
        out_specs=(
            pl.BlockSpec((own, rank, tile), lambda i: (0, 0, i)),
            pl.BlockSpec((own, rank, tile), lambda i: (0, 0, i)),
        ),
        compiler_params=pltpu.CompilerParams(vmem_limit_bytes=40 * 1024 * 1024),
        name="collect",
    )(slots, base, terms)
    return delta_t, grad_input_t, grad_down, grad_up


def solution(mesh):
    return jax.shard_map(
        functools.partial(shards, mesh.shape["dp"]),
        mesh=mesh,
        in_specs=(
            P("tensor", ("groups", "dp")),
            P("tensor", ("groups", "dp")),
            P(("groups", "dp"), None, "tensor"),
            P(("groups", "dp"), None, "tensor"),
            P(("groups", "dp")),
            P(("groups", "dp")),
            P("groups"),
        ),
        out_specs=(
            P("tensor", ("groups", "dp")),
            P("tensor", ("groups", "dp")),
            P(("groups", "dp"), None, "tensor"),
            P(("groups", "dp"), None, "tensor"),
        ),
        check_vma=False,
    )
```

```python
import functools
import jax
import jax.numpy as jnp
from jax import lax
from jax.experimental import pallas as pl
from jax.experimental.pallas import tpu as pltpu
from jax.sharding import PartitionSpec as P

MESH = pl.DeviceIdType.MESH
BF = jnp.bfloat16
F32 = jnp.float32
CHUNKS = 4
LANES = 4
WAYS = tuple(1 if w < LANES // 2 else -1 for w in range(LANES))


def place_of(dev, n):
    odd = lax.rem(dev, 2)
    half = lax.div(dev, 2)
    return (1 - odd) * half + odd * (n - 1 - half)


def dev_of(place, n):
    q = lax.rem(place + 2 * n, n)
    high = lax.div(q, n // 2)
    return (1 - high) * (2 * q) + high * (2 * (n - 1 - q) + 1)


def exchange(
    n,
    tenant_ref, rows_ref, owner_ref, in_hbm, cot_hbm, down_hbm, up_hbm,
    delta_hbm, gin_hbm, terms_hbm, slots_hbm,
    tokens, adapters, slot_src, slots, first, ready, moving, mine, part_mine, part_other, ranks, terms,
    result,
    load_sem, slot_send, slot_recv, rs_send, rs_recv, part_send, part_recv,
    ag_send, ag_recv, keep_sem, out_sem, slot_out, credit,
):
    own, rank, width = down_hbm.shape
    half = width // 2
    piece = width // LANES
    depth = moving.shape[2]
    d = lax.axis_index("dp")
    t = lax.axis_index("tensor")
    p = place_of(d, n)
    neighbour = (dev_of(p + 1, n), dev_of(p - 1, n))

    loads = [
        pltpu.make_async_copy(down_hbm, adapters.at[0], load_sem.at[0]),
        pltpu.make_async_copy(up_hbm, adapters.at[1], load_sem.at[1]),
        pltpu.make_async_copy(in_hbm, tokens.at[0], load_sem.at[2]),
        pltpu.make_async_copy(cot_hbm, tokens.at[1], load_sem.at[3]),
    ]
    for load in loads:
        load.start()

    barrier = pltpu.get_barrier_semaphore()

    def greet(i, _):
        pl.semaphore_signal(
            barrier, inc=1, device_id={"dp": lax.rem(d + i, n)}, device_id_type=MESH
        )
        return 0

    lax.fori_loop(1, n, greet, 0)
    pl.semaphore_signal(barrier, inc=1, device_id={"tensor": 1 - t}, device_id_type=MESH)
    my_slot = owner_ref[tenant_ref[0]]
    slot_vec = jnp.full((1, 128), my_slot, jnp.int32)
    slot_src[...] = slot_vec
    slots[d] = slot_vec
    pl.semaphore_wait(barrier, n)

    def slot_copy(i):
        to = lax.rem(d + i, n)
        return pltpu.make_async_remote_copy(
            src_ref=slot_src, dst_ref=slots.at[d],
            send_sem=slot_send.at[i], recv_sem=slot_recv.at[d],
            device_id={"dp": to}, device_id_type=MESH,
        )

    def slot_wait(i):
        who = lax.rem(d + i, n)
        return pltpu.make_async_remote_copy(
            src_ref=slot_src, dst_ref=slots.at[who],
            send_sem=slot_send.at[i], recv_sem=slot_recv.at[who],
            device_id={"dp": who}, device_id_type=MESH,
        )

    lax.fori_loop(1, n, lambda i, c: (slot_copy(i).start(), c)[1], 0)
    loads[0].wait()
    loads[1].wait()
    lax.fori_loop(1, n, lambda i, c: (slot_wait(i).wait_recv(), c)[1], 0)

    def masks(block):
        v = jnp.broadcast_to(slots[block], (rank, 128))
        return [
            jnp.where(v == d * own + j, 1.0, 0.0).astype(F32).astype(BF) for j in range(own)
        ]

    def cut(w):
        return slice(w * piece, (w + 1) * piece)

    def share(a, w, chosen):
        total = None
        for j in range(own):
            gate = jnp.concatenate([chosen[j]] * (piece // 128), axis=1)
            term = gate * adapters[a, j, :, cut(w)]
            total = term if total is None else total + term
        return total

    def prepare(step):
        blocks = [dev_of(p - way * (1 + step), n) for way in (1, -1)]
        chosen = [masks(block) for block in blocks]
        for a in range(2):
            for w in range(LANES):
                ready[a, w] = share(a, w, chosen[(1 - WAYS[w]) // 2])

    def target(w):
        return neighbour[(1 - WAYS[w]) // 2]

    def rs_copy(a, w, step, src):
        return pltpu.make_async_remote_copy(
            src_ref=src, dst_ref=moving.at[a, w, lax.rem(step, depth)],
            send_sem=rs_send.at[a, w, lax.rem(step, depth)],
            recv_sem=rs_recv.at[a, w, lax.rem(step, depth)],
            device_id={"dp": target(w)}, device_id_type=MESH,
        )

    for a in range(2):
        chosen = [masks(dev_of(p - way, n)) for way in (1, -1)]
        for w in range(LANES):
            first[a, w] = share(a, w, chosen[(1 - WAYS[w]) // 2])
            rs_copy(a, w, 0, first.at[a, w]).start()
    prepare(1)

    def rs_step(step, _):
        here = lax.rem(step - 1, depth)
        for a in range(2):
            for w in range(LANES):
                rs_copy(a, w, step - 1, first.at[a, w]).wait_recv()
                moving[a, w, here] = moving[a, w, here] + ready[a, w]
                if depth < n - 1:
                    rs_copy(a, w, step - 1, first.at[a, w]).wait_send()

                    @pl.when((step >= 2) & (step - 2 <= n - 2 - depth))
                    def _():
                        pl.semaphore_signal(
                            credit.at[a, w], inc=1,
                            device_id={"dp": neighbour[(1 + WAYS[w]) // 2]}, device_id_type=MESH,
                        )

                    @pl.when(step >= depth)
                    def _():
                        pl.semaphore_wait(credit.at[a, w], 1)

                rs_copy(a, w, step, moving.at[a, w, here]).start()
        prepare(step + 1)
        return 0

    lax.fori_loop(1, n - 1, rs_step, 0)

    lanes = lax.broadcasted_iota(jnp.int32, (rank, 128), 1)
    keep = jnp.where(lanes < rows_ref[0], 1.0, 0.0).astype(F32)
    loads[2].wait()
    loads[3].wait()

    def part_copy(a):
        return pltpu.make_async_remote_copy(
            src_ref=part_mine.at[a], dst_ref=part_other.at[a],
            send_sem=part_send.at[a], recv_sem=part_recv.at[a],
            device_id={"tensor": 1 - t}, device_id_type=MESH,
        )

    for a in range(2):
        for w in range(LANES):
            rs_copy(a, w, n - 2, first.at[a, w]).wait_recv()
            mine[a, :, cut(w)] = moving[a, w, (n - 2) % depth] + ready[a, w]
        part_mine[a] = jnp.dot(mine[a], tokens[a], preferred_element_type=F32)
        part_copy(a).start()

    def ag_piece(a, w, step):
        block = dev_of(p - WAYS[w] * step, n)
        held = terms.at[a, block, :, pl.ds(w * piece, piece)]
        return held

    def ag_copy(a, w, step):
        held = ag_piece(a, w, step)
        return pltpu.make_async_remote_copy(
            src_ref=held, dst_ref=held,
            send_sem=ag_send.at[a, w, step], recv_sem=ag_recv.at[a, w, step],
            device_id={"dp": target(w)}, device_id_type=MESH,
        )

    def ag_arrive(a, w, step):
        held = ag_piece(a, w, step + 1)
        return pltpu.make_async_remote_copy(
            src_ref=held, dst_ref=held,
            send_sem=ag_send.at[a, w, step], recv_sem=ag_recv.at[a, w, step],
            device_id={"dp": target(w)}, device_id_type=MESH,
        )

    def keep_copy(a, r, step):
        block = dev_of(p - (1 - 2 * r) * step, n)
        return pltpu.make_async_copy(
            terms.at[a, block, :, pl.ds(r * half, half)],
            terms_hbm.at[a, block, :, pl.ds(r * half, half)],
            keep_sem.at[a, r, step],
        )

    for a in range(2):
        part_copy(a).wait_recv()
        ranks[a] = ((part_mine[a] + part_other[a]) * keep).astype(BF)
        for w in range(LANES):
            terms[a, d, :, cut(w)] = lax.dot_general(
                ranks[a], tokens[1 - a, cut(w), :],
                (((1,), (1,)), ((), ())), preferred_element_type=F32,
            ).astype(BF)
            ag_copy(a, w, 0).start()
        for r in range(2):
            keep_copy(a, r, 0).start()

    size = width // CHUNKS

    def result_copy(a, i):
        at = pl.ds(i * size, size)
        return pltpu.make_async_copy(
            result.at[a, at], (delta_hbm, gin_hbm)[a].at[at], out_sem.at[a, i]
        )

    def result_chunk(i):
        at = slice(i * size, (i + 1) * size)
        for a in range(2):
            twice = ranks[a] + ranks[a]
            result[a, at, :] = lax.dot_general(
                mine[1 - a, :, at], twice,
                (((0,), (0,)), ((), ())), preferred_element_type=F32,
            ).astype(BF)
            result_copy(a, i).start()

    def ag_step(step):
        for a in range(2):
            for w in range(LANES):
                ag_arrive(a, w, step - 1).wait_recv()
                ag_copy(a, w, step).start()
            for r in range(2):
                keep_copy(a, r, step).start()

    result_chunk(0)
    early = min(CHUNKS, n - 1)
    for step in range(1, early):
        ag_step(step)
        result_chunk(step)
    for i in range(early, CHUNKS):
        result_chunk(i)
    lax.fori_loop(early, n - 1, lambda s, c: (ag_step(s), c)[1], 0)
    slot_keep = pltpu.make_async_copy(slots, slots_hbm, slot_out)
    slot_keep.start()
    for a in range(2):
        for w in range(LANES):
            ag_arrive(a, w, n - 2).wait_recv()
        for r in range(2):
            keep_copy(a, r, n - 1).start()

    def slot_end(i, c):
        slot_copy(i).wait_send()
        return c

    lax.fori_loop(1, n, slot_end, 0)

    def rs_end(step, c):
        for a in range(2):
            for w in range(LANES):
                rs_copy(a, w, step, first.at[a, w]).wait_send()
        return c

    lax.fori_loop(n - 2 if depth < n - 1 else 0, n - 1, rs_end, 0)

    def ag_end(step, c):
        for a in range(2):
            for w in range(LANES):
                ag_copy(a, w, step).wait_send()
        return c

    lax.fori_loop(0, n - 1, ag_end, 0)

    def keep_end(step, c):
        for a in range(2):
            for r in range(2):
                keep_copy(a, r, step).wait()
        return c

    lax.fori_loop(0, n, keep_end, 0)
    for a in range(2):
        part_copy(a).wait_send()
        for i in range(CHUNKS):
            result_copy(a, i).wait()
    slot_keep.wait()


def collect(n, slots_ref, base_ref, terms_ref, down_ref, up_ref):
    own = down_ref.shape[0]
    down_ref[...] = jnp.zeros_like(down_ref)
    up_ref[...] = jnp.zeros_like(up_ref)

    def add(b, c):
        at = slots_ref[b, 0, 0] - base_ref[0]

        @pl.when((at >= 0) & (at < own))
        def _():
            up_ref[at] += 0.125 * terms_ref[0, b].astype(F32)
            down_ref[at] += 0.125 * terms_ref[1, b].astype(F32)

        return c

    lax.fori_loop(0, n, add, 0)


def shards(n, inputs_t, cotangent_t, adapter_down, adapter_up, block_tenant, block_rows, owner_slot):
    width, columns = inputs_t.shape
    own, rank, _ = adapter_down.shape
    piece = width // LANES
    depth = min(n - 1, 8)
    smem = pl.BlockSpec(memory_space=pltpu.SMEM)
    anyw = pl.BlockSpec(memory_space=pl.ANY)
    dma = pltpu.SemaphoreType.DMA
    delta_t, grad_input_t, terms, slots = pl.pallas_call(
        functools.partial(exchange, n),
        out_shape=(
            jax.ShapeDtypeStruct((width, columns), BF),
            jax.ShapeDtypeStruct((width, columns), BF),
            jax.ShapeDtypeStruct((2, n, rank, width), BF),
            jax.ShapeDtypeStruct((n, 1, 128), jnp.int32),
        ),
        in_specs=[smem, smem, smem, anyw, anyw, anyw, anyw],
        out_specs=(anyw,) * 4,
        scratch_shapes=[
            pltpu.VMEM((2, width, columns), BF),
            pltpu.VMEM((2, own, rank, width), BF),
            pltpu.VMEM((1, 128), jnp.int32),
            pltpu.VMEM((n, 1, 128), jnp.int32),
            pltpu.VMEM((2, LANES, rank, piece), BF),
            pltpu.VMEM((2, LANES, rank, piece), BF),
            pltpu.VMEM((2, LANES, depth, rank, piece), BF),
            pltpu.VMEM((2, rank, width), BF),
            pltpu.VMEM((2, rank, columns), F32),
            pltpu.VMEM((2, rank, columns), F32),
            pltpu.VMEM((2, rank, columns), BF),
            pltpu.VMEM((2, n, rank, width), BF),
            pltpu.VMEM((2, width, columns), BF),
            dma((4,)),
            dma((n,)),
            dma((n,)),
            dma((2, LANES, depth)),
            dma((2, LANES, depth)),
            dma((2,)),
            dma((2,)),
            dma((2, LANES, n)),
            dma((2, LANES, n)),
            dma((2, 2, n)),
            dma((2, CHUNKS)),
            dma,
            pltpu.SemaphoreType.REGULAR((2, LANES)),
        ],
        compiler_params=pltpu.CompilerParams(
            collective_id=0, has_side_effects=True, vmem_limit_bytes=56 * 1024 * 1024
        ),
        name="exchange",
    )(block_tenant, block_rows, owner_slot, inputs_t, cotangent_t, adapter_down, adapter_up)
    base = jnp.full((1,), lax.axis_index("dp") * own, jnp.int32)
    tile = min(width, 1024)
    grad_down, grad_up = pl.pallas_call(
        functools.partial(collect, n),
        grid=(width // tile,),
        out_shape=(
            jax.ShapeDtypeStruct((own, rank, width), F32),
            jax.ShapeDtypeStruct((own, rank, width), F32),
        ),
        in_specs=[smem, smem, pl.BlockSpec((2, n, rank, tile), lambda i: (0, 0, 0, i))],
        out_specs=(
            pl.BlockSpec((own, rank, tile), lambda i: (0, 0, i)),
            pl.BlockSpec((own, rank, tile), lambda i: (0, 0, i)),
        ),
        compiler_params=pltpu.CompilerParams(vmem_limit_bytes=60 * 1024 * 1024),
        name="collect",
    )(slots, base, terms)
    return delta_t, grad_input_t, grad_down, grad_up


def solution(mesh):
    return jax.shard_map(
        functools.partial(shards, mesh.shape["dp"]),
        mesh=mesh,
        in_specs=(
            P("tensor", ("groups", "dp")),
            P("tensor", ("groups", "dp")),
            P(("groups", "dp"), None, "tensor"),
            P(("groups", "dp"), None, "tensor"),
            P(("groups", "dp")),
            P(("groups", "dp")),
            P("groups"),
        ),
        out_specs=(
            P("tensor", ("groups", "dp")),
            P("tensor", ("groups", "dp")),
            P(("groups", "dp"), None, "tensor"),
            P(("groups", "dp"), None, "tensor"),
        ),
        check_vma=False,
    )
```

```python
import functools
import jax
import jax.numpy as jnp
from jax import lax
from jax.experimental import pallas as pl
from jax.experimental.pallas import tpu as pltpu
from jax.sharding import PartitionSpec as P

MESH = pl.DeviceIdType.MESH
BF = jnp.bfloat16
F32 = jnp.float32
LANES = 4
WAYS = tuple(1 if w < LANES // 2 else -1 for w in range(LANES))


def place_of(dev, n):
    odd = lax.rem(dev, 2)
    half = lax.div(dev, 2)
    return (1 - odd) * half + odd * (n - 1 - half)


def dev_of(place, n):
    q = lax.rem(place + 2 * n, n)
    high = lax.div(q, n // 2)
    return (1 - high) * (2 * q) + high * (2 * (n - 1 - q) + 1)


def exchange(
    n,
    tenant_ref, rows_ref, owner_ref, in_hbm, cot_hbm, down_hbm, up_hbm,
    mine_hbm, ranks_hbm, terms_hbm, slots_hbm,
    tokens, adapters, slot_src, slots, first, ready, moving, mine, part_mine, part_other, ranks, terms,
    load_sem, slot_send, slot_recv, rs_send, rs_recv, part_send, part_recv,
    ag_send, ag_recv, keep_sem, out_sem, credit,
):
    own, rank, width = down_hbm.shape
    half = width // 2
    piece = width // LANES
    depth = moving.shape[2]
    d = lax.axis_index("dp")
    t = lax.axis_index("tensor")
    p = place_of(d, n)
    neighbour = (dev_of(p + 1, n), dev_of(p - 1, n))

    loads = [
        pltpu.make_async_copy(down_hbm, adapters.at[0], load_sem.at[0]),
        pltpu.make_async_copy(up_hbm, adapters.at[1], load_sem.at[1]),
        pltpu.make_async_copy(in_hbm, tokens.at[0], load_sem.at[2]),
        pltpu.make_async_copy(cot_hbm, tokens.at[1], load_sem.at[3]),
    ]
    for load in loads:
        load.start()

    barrier = pltpu.get_barrier_semaphore()

    def greet(i, _):
        pl.semaphore_signal(
            barrier, inc=1, device_id={"dp": lax.rem(d + i, n)}, device_id_type=MESH
        )
        return 0

    lax.fori_loop(1, n, greet, 0)
    pl.semaphore_signal(barrier, inc=1, device_id={"tensor": 1 - t}, device_id_type=MESH)
    my_slot = owner_ref[tenant_ref[0]]
    slot_vec = jnp.full((1, 128), my_slot, jnp.int32)
    slot_src[...] = slot_vec
    slots[d] = slot_vec
    pl.semaphore_wait(barrier, n)

    def slot_copy(i):
        to = lax.rem(d + i, n)
        return pltpu.make_async_remote_copy(
            src_ref=slot_src, dst_ref=slots.at[d],
            send_sem=slot_send.at[i], recv_sem=slot_recv.at[d],
            device_id={"dp": to}, device_id_type=MESH,
        )

    def slot_wait(i):
        who = lax.rem(d + i, n)
        return pltpu.make_async_remote_copy(
            src_ref=slot_src, dst_ref=slots.at[who],
            send_sem=slot_send.at[i], recv_sem=slot_recv.at[who],
            device_id={"dp": who}, device_id_type=MESH,
        )

    lax.fori_loop(1, n, lambda i, c: (slot_copy(i).start(), c)[1], 0)
    loads[0].wait()
    loads[1].wait()
    lax.fori_loop(1, n, lambda i, c: (slot_wait(i).wait_recv(), c)[1], 0)

    def masks(block):
        v = jnp.broadcast_to(slots[block], (rank, 128))
        return [
            jnp.where(v == d * own + j, 1.0, 0.0).astype(F32).astype(BF) for j in range(own)
        ]

    def cut(w):
        return slice(w * piece, (w + 1) * piece)

    def share(a, w, chosen):
        total = None
        for j in range(own):
            gate = jnp.concatenate([chosen[j]] * (piece // 128), axis=1)
            term = gate * adapters[a, j, :, cut(w)]
            total = term if total is None else total + term
        return total

    def prepare(step):
        blocks = [dev_of(p - way * (1 + step), n) for way in (1, -1)]
        chosen = [masks(block) for block in blocks]
        for a in range(2):
            for w in range(LANES):
                ready[a, w] = share(a, w, chosen[(1 - WAYS[w]) // 2])

    def target(w):
        return neighbour[(1 - WAYS[w]) // 2]

    def rs_copy(a, w, step, src):
        return pltpu.make_async_remote_copy(
            src_ref=src, dst_ref=moving.at[a, w, lax.rem(step, depth)],
            send_sem=rs_send.at[a, w, lax.rem(step, depth)],
            recv_sem=rs_recv.at[a, w, lax.rem(step, depth)],
            device_id={"dp": target(w)}, device_id_type=MESH,
        )

    for a in range(2):
        chosen = [masks(dev_of(p - way, n)) for way in (1, -1)]
        for w in range(LANES):
            first[a, w] = share(a, w, chosen[(1 - WAYS[w]) // 2])
            rs_copy(a, w, 0, first.at[a, w]).start()
    prepare(1)

    def rs_step(step, _):
        here = lax.rem(step - 1, depth)
        for a in range(2):
            for w in range(LANES):
                rs_copy(a, w, step - 1, first.at[a, w]).wait_recv()
                moving[a, w, here] = moving[a, w, here] + ready[a, w]
                if depth < n - 1:
                    rs_copy(a, w, step - 1, first.at[a, w]).wait_send()

                    @pl.when((step >= 2) & (step - 2 <= n - 2 - depth))
                    def _():
                        pl.semaphore_signal(
                            credit.at[a, w], inc=1,
                            device_id={"dp": neighbour[(1 + WAYS[w]) // 2]}, device_id_type=MESH,
                        )

                    @pl.when(step >= depth)
                    def _():
                        pl.semaphore_wait(credit.at[a, w], 1)

                rs_copy(a, w, step, moving.at[a, w, here]).start()
        prepare(step + 1)
        return 0

    lax.fori_loop(1, n - 1, rs_step, 0)

    lanes = lax.broadcasted_iota(jnp.int32, (rank, 128), 1)
    keep = jnp.where(lanes < rows_ref[0], 1.0, 0.0).astype(F32)
    loads[2].wait()
    loads[3].wait()

    def part_copy(a):
        return pltpu.make_async_remote_copy(
            src_ref=part_mine.at[a], dst_ref=part_other.at[a],
            send_sem=part_send.at[a], recv_sem=part_recv.at[a],
            device_id={"tensor": 1 - t}, device_id_type=MESH,
        )

    for a in range(2):
        for w in range(LANES):
            rs_copy(a, w, n - 2, first.at[a, w]).wait_recv()
            got = moving[a, w, (n - 2) % depth] + ready[a, w]
            mine[a, :, cut(w)] = got
            term = jnp.dot(got, tokens[a, cut(w), :], preferred_element_type=F32)
            part_mine[a] = term if w == 0 else part_mine[a] + term
        part_copy(a).start()

    def ag_piece(a, w, step):
        block = dev_of(p - WAYS[w] * step, n)
        held = terms.at[a, block, :, pl.ds(w * piece, piece)]
        return held

    def ag_copy(a, w, step):
        held = ag_piece(a, w, step)
        return pltpu.make_async_remote_copy(
            src_ref=held, dst_ref=held,
            send_sem=ag_send.at[a, w, step], recv_sem=ag_recv.at[a, w, step],
            device_id={"dp": target(w)}, device_id_type=MESH,
        )

    def ag_arrive(a, w, step):
        held = ag_piece(a, w, step + 1)
        return pltpu.make_async_remote_copy(
            src_ref=held, dst_ref=held,
            send_sem=ag_send.at[a, w, step], recv_sem=ag_recv.at[a, w, step],
            device_id={"dp": target(w)}, device_id_type=MESH,
        )

    def keep_copy(a, r, step):
        block = dev_of(p - (1 - 2 * r) * step, n)
        return pltpu.make_async_copy(
            terms.at[a, block, :, pl.ds(r * half, half)],
            terms_hbm.at[a, block, :, pl.ds(r * half, half)],
            keep_sem.at[a, r, step],
        )

    for a in range(2):
        part_copy(a).wait_recv()
        ranks[a] = ((part_mine[a] + part_other[a]) * keep).astype(BF)
        for w in range(LANES):
            terms[a, d, :, cut(w)] = lax.dot_general(
                ranks[a], tokens[1 - a, cut(w), :],
                (((1,), (1,)), ((), ())), preferred_element_type=F32,
            ).astype(BF)
            ag_copy(a, w, 0).start()
        for r in range(2):
            keep_copy(a, r, 0).start()

    outs = [
        pltpu.make_async_copy(mine, mine_hbm, out_sem.at[0]),
        pltpu.make_async_copy(ranks, ranks_hbm, out_sem.at[1]),
        pltpu.make_async_copy(slots, slots_hbm, out_sem.at[2]),
    ]
    for out in outs:
        out.start()

    def ag_step(step):
        for a in range(2):
            for w in range(LANES):
                ag_arrive(a, w, step - 1).wait_recv()
                ag_copy(a, w, step).start()
            for r in range(2):
                keep_copy(a, r, step).start()

    lax.fori_loop(1, n - 1, lambda k, c: (ag_step(k), c)[1], 0)
    for a in range(2):
        for w in range(LANES):
            ag_arrive(a, w, n - 2).wait_recv()
        for r in range(2):
            keep_copy(a, r, n - 1).start()

    def slot_end(i, c):
        slot_copy(i).wait_send()
        return c

    lax.fori_loop(1, n, slot_end, 0)

    def rs_end(step, c):
        for a in range(2):
            for w in range(LANES):
                rs_copy(a, w, step, first.at[a, w]).wait_send()
        return c

    lax.fori_loop(n - 2 if depth < n - 1 else 0, n - 1, rs_end, 0)

    def ag_end(step, c):
        for a in range(2):
            for w in range(LANES):
                ag_copy(a, w, step).wait_send()
        return c

    lax.fori_loop(0, n - 1, ag_end, 0)

    def keep_end(step, c):
        for a in range(2):
            for r in range(2):
                keep_copy(a, r, step).wait()
        return c

    lax.fori_loop(0, n, keep_end, 0)
    for a in range(2):
        part_copy(a).wait_send()
    for out in outs:
        out.wait()


def collect(
    n, slots_ref, base_ref, terms_ref, mine_ref, ranks_ref, delta_ref, gin_ref, down_ref, up_ref
):
    own = down_ref.shape[0]
    down_ref[...] = jnp.zeros_like(down_ref)
    up_ref[...] = jnp.zeros_like(up_ref)

    def add(b, c):
        at = slots_ref[b, 0, 0] - base_ref[0]

        @pl.when((at >= 0) & (at < own))
        def _():
            up_ref[at] += 0.125 * terms_ref[0, b].astype(F32)
            down_ref[at] += 0.125 * terms_ref[1, b].astype(F32)

        return c

    lax.fori_loop(0, n, add, 0)
    for a, out in enumerate((delta_ref, gin_ref)):
        out[...] = lax.dot_general(
            mine_ref[1 - a], ranks_ref[a] + ranks_ref[a],
            (((0,), (0,)), ((), ())), preferred_element_type=F32,
        ).astype(BF)


def shards(n, inputs_t, cotangent_t, adapter_down, adapter_up, block_tenant, block_rows, owner_slot):
    width, columns = inputs_t.shape
    own, rank, _ = adapter_down.shape
    piece = width // LANES
    depth = min(n - 1, 8)
    smem = pl.BlockSpec(memory_space=pltpu.SMEM)
    anyw = pl.BlockSpec(memory_space=pl.ANY)
    dma = pltpu.SemaphoreType.DMA
    mine, ranks, terms, slots = pl.pallas_call(
        functools.partial(exchange, n),
        out_shape=(
            jax.ShapeDtypeStruct((2, rank, width), BF),
            jax.ShapeDtypeStruct((2, rank, columns), BF),
            jax.ShapeDtypeStruct((2, n, rank, width), BF),
            jax.ShapeDtypeStruct((n, 1, 128), jnp.int32),
        ),
        in_specs=[smem, smem, smem, anyw, anyw, anyw, anyw],
        out_specs=(anyw,) * 4,
        scratch_shapes=[
            pltpu.VMEM((2, width, columns), BF),
            pltpu.VMEM((2, own, rank, width), BF),
            pltpu.VMEM((1, 128), jnp.int32),
            pltpu.VMEM((n, 1, 128), jnp.int32),
            pltpu.VMEM((2, LANES, rank, piece), BF),
            pltpu.VMEM((2, LANES, rank, piece), BF),
            pltpu.VMEM((2, LANES, depth, rank, piece), BF),
            pltpu.VMEM((2, rank, width), BF),
            pltpu.VMEM((2, rank, columns), F32),
            pltpu.VMEM((2, rank, columns), F32),
            pltpu.VMEM((2, rank, columns), BF),
            pltpu.VMEM((2, n, rank, width), BF),
            dma((4,)),
            dma((n,)),
            dma((n,)),
            dma((2, LANES, depth)),
            dma((2, LANES, depth)),
            dma((2,)),
            dma((2,)),
            dma((2, LANES, n)),
            dma((2, LANES, n)),
            dma((2, 2, n)),
            dma((3,)),
            pltpu.SemaphoreType.REGULAR((2, LANES)),
        ],
        compiler_params=pltpu.CompilerParams(
            collective_id=0, has_side_effects=True, vmem_limit_bytes=56 * 1024 * 1024
        ),
        name="exchange",
    )(block_tenant, block_rows, owner_slot, inputs_t, cotangent_t, adapter_down, adapter_up)
    base = jnp.full((1,), lax.axis_index("dp") * own, jnp.int32)
    tile = min(width, 2048)
    return pl.pallas_call(
        functools.partial(collect, n),
        grid=(width // tile,),
        out_shape=(
            jax.ShapeDtypeStruct((width, columns), BF),
            jax.ShapeDtypeStruct((width, columns), BF),
            jax.ShapeDtypeStruct((own, rank, width), F32),
            jax.ShapeDtypeStruct((own, rank, width), F32),
        ),
        in_specs=[
            smem,
            smem,
            pl.BlockSpec((2, n, rank, tile), lambda i: (0, 0, 0, i)),
            pl.BlockSpec((2, rank, tile), lambda i: (0, 0, i)),
            pl.BlockSpec((2, rank, columns), lambda i: (0, 0, 0)),
        ],
        out_specs=(
            pl.BlockSpec((tile, columns), lambda i: (i, 0)),
            pl.BlockSpec((tile, columns), lambda i: (i, 0)),
            pl.BlockSpec((own, rank, tile), lambda i: (0, 0, i)),
            pl.BlockSpec((own, rank, tile), lambda i: (0, 0, i)),
        ),
        compiler_params=pltpu.CompilerParams(vmem_limit_bytes=60 * 1024 * 1024),
        name="collect",
    )(slots, base, terms, mine, ranks)


def solution(mesh):
    return jax.shard_map(
        functools.partial(shards, mesh.shape["dp"]),
        mesh=mesh,
        in_specs=(
            P("tensor", ("groups", "dp")),
            P("tensor", ("groups", "dp")),
            P(("groups", "dp"), None, "tensor"),
            P(("groups", "dp"), None, "tensor"),
            P(("groups", "dp")),
            P(("groups", "dp")),
            P("groups"),
        ),
        out_specs=(
            P("tensor", ("groups", "dp")),
            P("tensor", ("groups", "dp")),
            P(("groups", "dp"), None, "tensor"),
            P(("groups", "dp"), None, "tensor"),
        ),
        check_vma=False,
    )
```

```python
import functools
import jax
import jax.numpy as jnp
from jax import lax
from jax.experimental import pallas as pl
from jax.experimental.pallas import tpu as pltpu
from jax.sharding import PartitionSpec as P

MESH = pl.DeviceIdType.MESH
BF = jnp.bfloat16
F32 = jnp.float32
LANES = 4
WAYS = tuple(1 if w < LANES // 2 else -1 for w in range(LANES))
ORDER = tuple(w // 2 + (w % 2) * (LANES // 2) for w in range(LANES))


def place_of(dev, n):
    odd = lax.rem(dev, 2)
    half = lax.div(dev, 2)
    return (1 - odd) * half + odd * (n - 1 - half)


def dev_of(place, n):
    q = lax.rem(place + 2 * n, n)
    high = lax.div(q, n // 2)
    return (1 - high) * (2 * q) + high * (2 * (n - 1 - q) + 1)


def exchange(
    n,
    tenant_ref, rows_ref, owner_ref, in_hbm, cot_hbm, down_hbm, up_hbm,
    mine_hbm, ranks_hbm, terms_hbm, slots_hbm,
    tokens, adapters, slot_src, slots, first, ready, moving, mine, part_mine, part_other, ranks, terms,
    load_sem, slot_send, slot_recv, rs_send, rs_recv, part_send, part_recv,
    ag_send, ag_recv, keep_sem, out_sem, credit,
):
    own, rank, width = down_hbm.shape
    half = width // 2
    piece = width // LANES
    depth = moving.shape[2]
    d = lax.axis_index("dp")
    t = lax.axis_index("tensor")
    p = place_of(d, n)
    neighbour = (dev_of(p + 1, n), dev_of(p - 1, n))

    loads = [
        pltpu.make_async_copy(down_hbm, adapters.at[0], load_sem.at[0]),
        pltpu.make_async_copy(up_hbm, adapters.at[1], load_sem.at[1]),
        pltpu.make_async_copy(in_hbm, tokens.at[0], load_sem.at[2]),
        pltpu.make_async_copy(cot_hbm, tokens.at[1], load_sem.at[3]),
    ]
    for load in loads:
        load.start()

    barrier = pltpu.get_barrier_semaphore()

    def greet(i, _):
        pl.semaphore_signal(
            barrier, inc=1, device_id={"dp": lax.rem(d + i, n)}, device_id_type=MESH
        )
        return 0

    lax.fori_loop(1, n, greet, 0)
    pl.semaphore_signal(barrier, inc=1, device_id={"tensor": 1 - t}, device_id_type=MESH)
    my_slot = owner_ref[tenant_ref[0]]
    slot_vec = jnp.full((1, 128), my_slot, jnp.int32)
    slot_src[...] = slot_vec
    slots[d] = slot_vec
    pl.semaphore_wait(barrier, n)

    def slot_copy(i):
        to = lax.rem(d + i, n)
        return pltpu.make_async_remote_copy(
            src_ref=slot_src, dst_ref=slots.at[d],
            send_sem=slot_send.at[i], recv_sem=slot_recv.at[d],
            device_id={"dp": to}, device_id_type=MESH,
        )

    def slot_wait(i):
        who = lax.rem(d + i, n)
        return pltpu.make_async_remote_copy(
            src_ref=slot_src, dst_ref=slots.at[who],
            send_sem=slot_send.at[i], recv_sem=slot_recv.at[who],
            device_id={"dp": who}, device_id_type=MESH,
        )

    lax.fori_loop(1, n, lambda i, c: (slot_copy(i).start(), c)[1], 0)
    loads[0].wait()
    loads[1].wait()
    lax.fori_loop(1, n, lambda i, c: (slot_wait(i).wait_recv(), c)[1], 0)

    def masks(block):
        v = jnp.broadcast_to(slots[block], (rank, 128))
        return [
            jnp.where(v == d * own + j, 1.0, 0.0).astype(F32).astype(BF) for j in range(own)
        ]

    def cut(w):
        return slice(w * piece, (w + 1) * piece)

    def share(a, w, chosen):
        total = None
        for j in range(own):
            gate = jnp.concatenate([chosen[j]] * (piece // 128), axis=1)
            term = gate * adapters[a, j, :, cut(w)]
            total = term if total is None else total + term
        return total

    def prepare(step):
        blocks = [dev_of(p - way * (1 + step), n) for way in (1, -1)]
        chosen = [masks(block) for block in blocks]
        for a in range(2):
            for w in ORDER:
                ready[a, w] = share(a, w, chosen[(1 - WAYS[w]) // 2])

    def target(w):
        return neighbour[(1 - WAYS[w]) // 2]

    def rs_copy(a, w, step, src):
        return pltpu.make_async_remote_copy(
            src_ref=src, dst_ref=moving.at[a, w, lax.rem(step, depth)],
            send_sem=rs_send.at[a, w, lax.rem(step, depth)],
            recv_sem=rs_recv.at[a, w, lax.rem(step, depth)],
            device_id={"dp": target(w)}, device_id_type=MESH,
        )

    for a in range(2):
        chosen = [masks(dev_of(p - way, n)) for way in (1, -1)]
        for w in ORDER:
            first[a, w] = share(a, w, chosen[(1 - WAYS[w]) // 2])
            rs_copy(a, w, 0, first.at[a, w]).start()
    prepare(1)

    def rs_step(step, _):
        here = lax.rem(step - 1, depth)
        for a in range(2):
            for w in ORDER:
                rs_copy(a, w, step - 1, first.at[a, w]).wait_recv()
                moving[a, w, here] = moving[a, w, here] + ready[a, w]
                if depth < n - 1:
                    rs_copy(a, w, step - 1, first.at[a, w]).wait_send()

                    @pl.when((step >= 2) & (step - 2 <= n - 2 - depth))
                    def _():
                        pl.semaphore_signal(
                            credit.at[a, w], inc=1,
                            device_id={"dp": neighbour[(1 + WAYS[w]) // 2]}, device_id_type=MESH,
                        )

                    @pl.when(step >= depth)
                    def _():
                        pl.semaphore_wait(credit.at[a, w], 1)

                rs_copy(a, w, step, moving.at[a, w, here]).start()
        prepare(step + 1)
        return 0

    lax.fori_loop(1, n - 1, rs_step, 0)

    lanes = lax.broadcasted_iota(jnp.int32, (rank, 128), 1)
    keep = jnp.where(lanes < rows_ref[0], 1.0, 0.0).astype(F32)
    loads[2].wait()
    loads[3].wait()

    def part_copy(a):
        return pltpu.make_async_remote_copy(
            src_ref=part_mine.at[a], dst_ref=part_other.at[a],
            send_sem=part_send.at[a], recv_sem=part_recv.at[a],
            device_id={"tensor": 1 - t}, device_id_type=MESH,
        )

    for a in range(2):
        for w in ORDER:
            rs_copy(a, w, n - 2, first.at[a, w]).wait_recv()
            got = moving[a, w, (n - 2) % depth] + ready[a, w]
            mine[a, :, cut(w)] = got
            term = jnp.dot(got, tokens[a, cut(w), :], preferred_element_type=F32)
            part_mine[a] = term if w == 0 else part_mine[a] + term
        part_copy(a).start()

    def ag_piece(a, w, step):
        block = dev_of(p - WAYS[w] * step, n)
        held = terms.at[a, block, :, pl.ds(w * piece, piece)]
        return held

    def ag_copy(a, w, step):
        held = ag_piece(a, w, step)
        return pltpu.make_async_remote_copy(
            src_ref=held, dst_ref=held,
            send_sem=ag_send.at[a, w, step], recv_sem=ag_recv.at[a, w, step],
            device_id={"dp": target(w)}, device_id_type=MESH,
        )

    def ag_arrive(a, w, step):
        held = ag_piece(a, w, step + 1)
        return pltpu.make_async_remote_copy(
            src_ref=held, dst_ref=held,
            send_sem=ag_send.at[a, w, step], recv_sem=ag_recv.at[a, w, step],
            device_id={"dp": target(w)}, device_id_type=MESH,
        )

    def keep_copy(a, r, step):
        block = dev_of(p - (1 - 2 * r) * step, n)
        return pltpu.make_async_copy(
            terms.at[a, block, :, pl.ds(r * half, half)],
            terms_hbm.at[a, block, :, pl.ds(r * half, half)],
            keep_sem.at[a, r, step],
        )

    for a in range(2):
        part_copy(a).wait_recv()
        ranks[a] = ((part_mine[a] + part_other[a]) * keep).astype(BF)
        for w in ORDER:
            terms[a, d, :, cut(w)] = lax.dot_general(
                ranks[a], tokens[1 - a, cut(w), :],
                (((1,), (1,)), ((), ())), preferred_element_type=F32,
            ).astype(BF)
            ag_copy(a, w, 0).start()
        for r in range(2):
            keep_copy(a, r, 0).start()

    outs = [
        pltpu.make_async_copy(mine, mine_hbm, out_sem.at[0]),
        pltpu.make_async_copy(ranks, ranks_hbm, out_sem.at[1]),
        pltpu.make_async_copy(slots, slots_hbm, out_sem.at[2]),
    ]
    for out in outs:
        out.start()

    def ag_step(step):
        for a in range(2):
            for w in ORDER:
                ag_arrive(a, w, step - 1).wait_recv()
                ag_copy(a, w, step).start()
            for r in range(2):
                keep_copy(a, r, step).start()

    lax.fori_loop(1, n - 1, lambda k, c: (ag_step(k), c)[1], 0)
    for a in range(2):
        for w in ORDER:
            ag_arrive(a, w, n - 2).wait_recv()
        for r in range(2):
            keep_copy(a, r, n - 1).start()

    def slot_end(i, c):
        slot_copy(i).wait_send()
        return c

    lax.fori_loop(1, n, slot_end, 0)

    def rs_end(step, c):
        for a in range(2):
            for w in ORDER:
                rs_copy(a, w, step, first.at[a, w]).wait_send()
        return c

    lax.fori_loop(n - 2 if depth < n - 1 else 0, n - 1, rs_end, 0)

    def ag_end(step, c):
        for a in range(2):
            for w in ORDER:
                ag_copy(a, w, step).wait_send()
        return c

    lax.fori_loop(0, n - 1, ag_end, 0)

    def keep_end(step, c):
        for a in range(2):
            for r in range(2):
                keep_copy(a, r, step).wait()
        return c

    lax.fori_loop(0, n, keep_end, 0)
    for a in range(2):
        part_copy(a).wait_send()
    for out in outs:
        out.wait()


def collect(
    n, slots_ref, base_ref, terms_ref, mine_ref, ranks_ref, delta_ref, gin_ref, down_ref, up_ref
):
    own = down_ref.shape[0]
    down_ref[...] = jnp.zeros_like(down_ref)
    up_ref[...] = jnp.zeros_like(up_ref)

    def add(b, c):
        at = slots_ref[b, 0, 0] - base_ref[0]

        @pl.when((at >= 0) & (at < own))
        def _():
            up_ref[at] += 0.125 * terms_ref[0, b].astype(F32)
            down_ref[at] += 0.125 * terms_ref[1, b].astype(F32)

        return c

    lax.fori_loop(0, n, add, 0, unroll=min(n, 8))
    for a, out in enumerate((delta_ref, gin_ref)):
        out[...] = lax.dot_general(
            mine_ref[1 - a], ranks_ref[a] + ranks_ref[a],
            (((0,), (0,)), ((), ())), preferred_element_type=F32,
        ).astype(BF)


def shards(n, inputs_t, cotangent_t, adapter_down, adapter_up, block_tenant, block_rows, owner_slot):
    width, columns = inputs_t.shape
    own, rank, _ = adapter_down.shape
    piece = width // LANES
    depth = min(n - 1, 8)
    smem = pl.BlockSpec(memory_space=pltpu.SMEM)
    anyw = pl.BlockSpec(memory_space=pl.ANY)
    dma = pltpu.SemaphoreType.DMA
    mine, ranks, terms, slots = pl.pallas_call(
        functools.partial(exchange, n),
        out_shape=(
            jax.ShapeDtypeStruct((2, rank, width), BF),
            jax.ShapeDtypeStruct((2, rank, columns), BF),
            jax.ShapeDtypeStruct((2, n, rank, width), BF),
            jax.ShapeDtypeStruct((n, 1, 128), jnp.int32),
        ),
        in_specs=[smem, smem, smem, anyw, anyw, anyw, anyw],
        out_specs=(anyw,) * 4,
        scratch_shapes=[
            pltpu.VMEM((2, width, columns), BF),
            pltpu.VMEM((2, own, rank, width), BF),
            pltpu.VMEM((1, 128), jnp.int32),
            pltpu.VMEM((n, 1, 128), jnp.int32),
            pltpu.VMEM((2, LANES, rank, piece), BF),
            pltpu.VMEM((2, LANES, rank, piece), BF),
            pltpu.VMEM((2, LANES, depth, rank, piece), BF),
            pltpu.VMEM((2, rank, width), BF),
            pltpu.VMEM((2, rank, columns), F32),
            pltpu.VMEM((2, rank, columns), F32),
            pltpu.VMEM((2, rank, columns), BF),
            pltpu.VMEM((2, n, rank, width), BF),
            dma((4,)),
            dma((n,)),
            dma((n,)),
            dma((2, LANES, depth)),
            dma((2, LANES, depth)),
            dma((2,)),
            dma((2,)),
            dma((2, LANES, n)),
            dma((2, LANES, n)),
            dma((2, 2, n)),
            dma((3,)),
            pltpu.SemaphoreType.REGULAR((2, LANES)),
        ],
        compiler_params=pltpu.CompilerParams(
            collective_id=0, has_side_effects=True, vmem_limit_bytes=56 * 1024 * 1024
        ),
        name="exchange",
    )(block_tenant, block_rows, owner_slot, inputs_t, cotangent_t, adapter_down, adapter_up)
    base = jnp.full((1,), lax.axis_index("dp") * own, jnp.int32)
    tile = min(width, 2048)
    return pl.pallas_call(
        functools.partial(collect, n),
        grid=(width // tile,),
        out_shape=(
            jax.ShapeDtypeStruct((width, columns), BF),
            jax.ShapeDtypeStruct((width, columns), BF),
            jax.ShapeDtypeStruct((own, rank, width), F32),
            jax.ShapeDtypeStruct((own, rank, width), F32),
        ),
        in_specs=[
            smem,
            smem,
            pl.BlockSpec((2, n, rank, tile), lambda i: (0, 0, 0, i)),
            pl.BlockSpec((2, rank, tile), lambda i: (0, 0, i)),
            pl.BlockSpec((2, rank, columns), lambda i: (0, 0, 0)),
        ],
        out_specs=(
            pl.BlockSpec((tile, columns), lambda i: (i, 0)),
            pl.BlockSpec((tile, columns), lambda i: (i, 0)),
            pl.BlockSpec((own, rank, tile), lambda i: (0, 0, i)),
            pl.BlockSpec((own, rank, tile), lambda i: (0, 0, i)),
        ),
        compiler_params=pltpu.CompilerParams(vmem_limit_bytes=60 * 1024 * 1024),
        name="collect",
    )(slots, base, terms, mine, ranks)


def solution(mesh):
    return jax.shard_map(
        functools.partial(shards, mesh.shape["dp"]),
        mesh=mesh,
        in_specs=(
            P("tensor", ("groups", "dp")),
            P("tensor", ("groups", "dp")),
            P(("groups", "dp"), None, "tensor"),
            P(("groups", "dp"), None, "tensor"),
            P(("groups", "dp")),
            P(("groups", "dp")),
            P("groups"),
        ),
        out_specs=(
            P("tensor", ("groups", "dp")),
            P("tensor", ("groups", "dp")),
            P(("groups", "dp"), None, "tensor"),
            P(("groups", "dp"), None, "tensor"),
        ),
        check_vma=False,
    )
```
